32 devices in a mesh: grp: 2 (over x), ex: 4 (over y, core), feat: 4 (over z).
Axes of the slice: x: 2, y: 2, z: 4, core: 2. Of those that a mesh axis runs over, the one named last changes fastest.
Arguments:
- queries: bfloat16 [640, 16384], P(('grp', 'ex'), 'feat'), parts along dimension 0, may hold values from -6 to 6
- train_grads: bfloat16 [8192, 16384], P(('grp', 'ex'), 'feat'), parts along dimension 0, may hold values from -6 to 6
- preconditioner: bfloat16 [8, 2048, 2048], P('feat', 'ex'), as said below
- query_ids: int32 [640], P(('grp', 'feat')), parts along dimension 0, may hold values from 0 to 4095
- train_ids: int32 [8192], P(('grp', 'ex')), parts along dimension 0, may hold values from 0 to 4095, each once
- layer_seeds: int32 [8], P('feat'), may hold values from 0 to 1073741823
Outputs:
- scores: float32 [640, 4096], P(('grp', 'feat'), 'ex'), parts along dimension 0
The draws below stay inside these ranges and needn't reach their ends.
There are 2 independent parts, one for each index of `grp`. The reference program is written for one: setup_inputs(seed, part) draws one part's arguments, and reference() takes and returns one part's arrays. A program takes and returns all parts, laid end to end along the dimension named above; an argument that names none is the same for every part. Nothing has to cross between parts.
Inputs may be any that keep to these rules, and one draw needn't show every extreme that they name: preconditioner[l] is symmetric for every layer. `train_ids`: each training example id appears once in the slab. `query_ids`: every query id is the id of some training example of the slab.
All inputs are finite; a program needn't handle non-finite values.
Results may differ from the reference program's by a relative error of at most 0.003.
Values may be sent and summed in bfloat16 or wider, within the bound.
A program may use at most 128 MiB of HBM per device.

```python
import math
import jax
import jax.numpy as jnp
from jax import lax

K = 2048
TR_DEV = 1024
LAYERS = 8
NQ = 320
NTR = 4096
N_EX = 4


def draw_preconditioner(key, part):
    key = jax.random.fold_in(key, 11)
    first_key, second_key = jax.random.split(key)
    diagonal = jnp.exp(jax.random.uniform(first_key, (LAYERS, K), jnp.float32, math.log(0.3), math.log(3.0)))
    jitter = jax.random.normal(second_key, (LAYERS, K, K), jnp.float32)
    symmetric = (jitter + jnp.swapaxes(jitter, 1, 2)) * (0.5 / math.sqrt(2.0 * K))
    root_scale = jnp.sqrt(diagonal)
    coupling = root_scale[:, :, None] * root_scale[:, None, :] * symmetric
    identity = (jnp.arange(K)[:, None] == jnp.arange(K)[None, :]).astype(jnp.float32)
    return (coupling + diagonal[:, :, None] * identity[None, :, :]).astype(jnp.bfloat16)


def touch_ends(result, key, smallest, largest):
    spot = [jax.random.randint(jax.random.fold_in(key, axis), (), 0, length) for axis, length in enumerate(result.shape)]
    widest = result.shape.index(max(result.shape))
    neighbour = spot[:widest] + [(spot[widest] + 1) % result.shape[widest]] + spot[widest + 1:]
    return result.at[tuple(spot)].set(smallest).at[tuple(neighbour)].set(largest)


def level_of(stream_key, extent, shards, smallest, top_value):
    def one(position, shards_of):
        heights = jax.random.uniform(jax.random.fold_in(jax.random.fold_in(stream_key, 6), position), (shards_of,), jnp.float32, smallest / len(shards), top_value / len(shards))
        return jnp.repeat(jnp.exp(heights), extent[position] // shards_of).reshape((-1,) + (1,) * (len(extent) - position - 1))

    loudness = one(*shards[0])
    for cut in shards[1:]:
        loudness = loudness * one(*cut)
    return loudness


def scatter_about(stream_key, extent, width, limit, cuts=(), held_as=jnp.bfloat16):
    gain = level_of(stream_key, extent, cuts, -0.22, 0.18) if cuts else 1.0
    values = jax.random.normal(stream_key, extent, jnp.float32) * width * gain
    return jnp.minimum(jnp.maximum(values, -limit), limit).astype(held_as)


def setup_inputs(seed: int = 0, part: int = 0) -> dict:
    arg_keys = jax.random.split(jax.random.key(seed), 7)
    part_keys = jax.random.split(jax.random.fold_in(arg_keys[6], part), 7)
    return {
        "queries": scatter_about(part_keys[0], (NQ, LAYERS * K), 1.0, 6.0, ((0, 4), (1, 4))),
        "train_grads": scatter_about(part_keys[1], (NTR, LAYERS * K), 1.0, 6.0, ((0, 4), (1, 4))),
        "preconditioner": draw_preconditioner(jax.random.fold_in(arg_keys[6], 71), part),
        "query_ids": touch_ends(jax.random.randint(part_keys[3], (NQ,), 0, TR_DEV * N_EX), jax.random.fold_in(part_keys[3], 1), 0, (TR_DEV * N_EX) - 1).astype(jnp.int32),
        "train_ids": jax.random.permutation(part_keys[4], TR_DEV * N_EX).astype(jnp.int32),
        "layer_seeds": touch_ends(jax.random.randint(arg_keys[5], (LAYERS,), 0, 1073741824), jax.random.fold_in(arg_keys[5], 1), 0, 1073741823).astype(jnp.int32),
    }


def sketch_signs(seed_values, feature_count):
    feature_index = jnp.arange(feature_count, dtype=jnp.int32)
    hashed = seed_values[:, None].astype(jnp.int32) + feature_index[None, :] * 40503
    hashed = (hashed ^ lax.shift_right_logical(hashed, jnp.full_like(hashed, 16))) * 73244475
    hashed = (hashed ^ lax.shift_right_logical(hashed, jnp.full_like(hashed, 16))) * 73244475
    hashed = hashed ^ lax.shift_right_logical(hashed, jnp.full_like(hashed, 16))
    return 1 - 2 * (hashed & 1)

def reference(queries, train_grads, preconditioner, query_ids, train_ids, layer_seeds):
    sign_flips = sketch_signs(layer_seeds, K).reshape(-1).astype(jnp.bfloat16)
    signed_rows = queries * sign_flips[None, :]

    def per_layer(running, index):
        start_col = index * K
        query_block = lax.dynamic_slice_in_dim(signed_rows, start_col, K, 1).astype(jnp.float32)
        weights = preconditioner[index].astype(jnp.float32)
        conditioned = jnp.dot(query_block, weights, precision=lax.Precision.HIGHEST).astype(jnp.bfloat16)
        conditioned = lax.optimization_barrier(conditioned).astype(jnp.float32)
        train_block = lax.dynamic_slice_in_dim(train_grads, start_col, K, 1).astype(jnp.float32)
        running = running + jnp.dot(conditioned, train_block.T, precision=lax.Precision.HIGHEST)
        return (running, None)
    initial = jnp.zeros((NQ, NTR), jnp.float32)
    accum_scores, _ = lax.scan(per_layer, initial, jnp.arange(LAYERS, dtype=jnp.int32))
    scaled = accum_scores * (1.0 / math.sqrt(LAYERS * K))
    self_match = query_ids[:, None] == train_ids[None, :]
    return jnp.where(self_match, jnp.float32(0.0), scaled)
```

```python
import functools
import math

import jax
import jax.numpy as jnp
from jax import lax
from jax.experimental import pallas as pl
from jax.experimental.pallas import tpu as pltpu
from jax.sharding import PartitionSpec as P

CHUNK = 16
TILE = 256
NT = (((1,), (1,)), ((), ()))


def sketch_sign_row(seed, width):
    feature = lax.broadcasted_iota(jnp.int32, (1, width), 1)
    hashed = seed + feature * 40503
    sixteen = jnp.full_like(hashed, 16)
    hashed = (hashed ^ lax.shift_right_logical(hashed, sixteen)) * 73244475
    hashed = (hashed ^ lax.shift_right_logical(hashed, sixteen)) * 73244475
    hashed = hashed ^ lax.shift_right_logical(hashed, sixteen)
    return (1 - 2 * (hashed & 1)).astype(jnp.float32).astype(jnp.bfloat16)


def kernel(
    n_ex, n_feat,
    q_hbm, g_hbm, p_hbm, qid_ref, tid_ref, seed_ref, out_ref,
    qbuf, cbuf, gbuf, pbuf, sbuf, zbuf, own, qcol,
    load_q, load_p, load_g,
    q_sib_s, q_sib_r, q_y_s, q_y_r, q_fw_s, q_fw_r,
    c_sib_s, c_sib_r, c_y_s, c_y_r, c_fw_s, c_fw_r,
    z_s, z_r,
):
    rows, feats = q_hbm.shape
    layers, prow, width = p_hbm.shape
    train = g_hbm.shape[0]
    steps = rows // CHUNK
    part = layers * prow
    per_owner = n_ex // n_feat
    far = n_ex // 2 - 1
    me = lax.axis_index("ex")
    fe = lax.axis_index("feat")
    sib = me + 1 - 2 * lax.rem(me, 2)

    def block(k, e):
        return qbuf.at[k, pl.ds(pl.multiple_of(e * CHUNK, CHUNK), CHUNK)]

    def columns(e):
        return pl.ds(pl.multiple_of(e * part, 128), part)

    def ahead(j):
        return lax.rem(me + 2 * j, n_ex)

    def behind(e, j):
        return lax.rem(e + n_ex - 2 * j, n_ex)

    def remote(ref, send, recv, target):
        return pltpu.make_async_remote_copy(
            src_ref=ref, dst_ref=ref, send_sem=send, recv_sem=recv,
            device_id={"ex": target}, device_id_type=pl.DeviceIdType.MESH,
        )

    q_loads = [
        pltpu.make_async_copy(q_hbm.at[pl.ds(k * CHUNK, CHUNK)], block(k, me), load_q.at[k])
        for k in range(steps)
    ]
    p_loads = [
        pltpu.make_async_copy(p_hbm.at[l], pbuf.at[l], load_p.at[l]) for l in range(layers)
    ]
    g_loads = [
        pltpu.make_async_copy(
            g_hbm.at[:, pl.ds(l * width + e * prow, prow)],
            gbuf.at[:, pl.ds(e * part + l * prow, prow)],
            load_g.at[e * layers + l],
        )
        for e in range(n_ex)
        for l in range(layers)
    ]
    for copy in q_loads + p_loads + g_loads:
        copy.start()

    barrier = pltpu.get_barrier_semaphore()
    pl.semaphore_signal(barrier, inc=1, device_id={"ex": sib}, device_id_type=pl.DeviceIdType.MESH)
    for j in range(1, far + 1):
        pl.semaphore_signal(barrier, inc=1, device_id={"ex": ahead(j)}, device_id_type=pl.DeviceIdType.MESH)
    for d in range(1, n_feat):
        pl.semaphore_signal(
            barrier, inc=1, device_id={"feat": lax.rem(fe + d, n_feat)}, device_id_type=pl.DeviceIdType.MESH
        )

    signs = [sketch_sign_row(seed_ref[l], width) for l in range(layers)]
    eye = lax.broadcasted_iota(jnp.int32, (qid_ref.shape[1],) * 2, 0) == lax.broadcasted_iota(
        jnp.int32, (qid_ref.shape[1],) * 2, 1
    )
    ids = jnp.broadcast_to(qid_ref[...].astype(jnp.float32), eye.shape)
    qcol[...] = jnp.broadcast_to(
        jnp.sum(jnp.where(eye, ids, 0.0), axis=1, keepdims=True), qcol.shape
    )

    sent = []

    def go(copy):
        copy.start()
        sent.append(copy)

    for k in range(steps):
        q_loads[k].wait()
        place = pl.ds(pl.multiple_of(me * CHUNK, CHUNK), CHUNK)
        for l in range(layers):
            lanes = slice(l * width, (l + 1) * width)
            qbuf[k, place, lanes] = qbuf[k, place, lanes] * signs[l]
        if k == 0:
            pl.semaphore_wait(barrier, far + n_feat)
        for j in range(1, far + 1):
            go(remote(block(k, me), q_y_s.at[j - 1, k], q_y_r.at[j - 1, k], ahead(j)))
        go(remote(block(k, me), q_sib_s.at[k], q_sib_r.at[k], sib))

    for k in range(steps):
        for j in range(1, far + 1):
            src = behind(me, j)
            remote(block(k, src), q_y_s.at[j - 1, k], q_y_r.at[j - 1, k], ahead(j)).wait_recv()
            go(remote(block(k, src), q_fw_s.at[j - 1, k], q_fw_r.at[j - 1, k], sib))
        remote(block(k, sib), q_sib_s.at[k], q_sib_r.at[k], sib).wait_recv()
        for j in range(1, far + 1):
            src = behind(sib, j)
            remote(block(k, src), q_fw_s.at[j - 1, k], q_fw_r.at[j - 1, k], sib).wait_recv()
        if k == 0:
            for copy in p_loads:
                copy.wait()
        for l in range(layers):
            got = lax.dot_general(
                qbuf[k, :, l * width:(l + 1) * width], pbuf[l], NT, preferred_element_type=jnp.float32
            )
            cbuf[k, :, pl.ds(pl.multiple_of(me * part + l * prow, 128), prow)] = got.astype(jnp.bfloat16)
        mine = cbuf.at[k, :, columns(me)]
        for j in range(1, far + 1):
            go(remote(mine, c_y_s.at[j - 1, k], c_y_r.at[j - 1, k], ahead(j)))
        go(remote(mine, c_sib_s.at[k], c_sib_r.at[k], sib))

    normal = 1.0 / math.sqrt(n_feat * layers * width)

    def z_copy(k, b):
        owner, spot = b // per_owner, (b % per_owner) * steps + k
        return pltpu.make_async_remote_copy(
            src_ref=sbuf.at[k, pl.ds(b * CHUNK, CHUNK)],
            dst_ref=zbuf.at[fe, pl.ds(spot * CHUNK, CHUNK)],
            send_sem=z_s.at[k, b],
            recv_sem=z_r.at[fe, spot],
            device_id={"feat": owner},
            device_id_type=pl.DeviceIdType.MESH,
        )

    def finish(k):
        for m in range(per_owner):
            spot = m * steps + k
            band = pl.ds(spot * CHUNK, CHUNK)
            total = own[band, :]
            for d in range(1, n_feat):
                src = lax.rem(fe + d, n_feat)
                pltpu.make_async_remote_copy(
                    src_ref=zbuf.at[src, band], dst_ref=zbuf.at[src, band],
                    send_sem=z_s.at[k, m], recv_sem=z_r.at[src, spot],
                    device_id={"feat": src}, device_id_type=pl.DeviceIdType.MESH,
                ).wait_recv()
                total = total + zbuf[src, band, :].astype(jnp.float32)
            same = qcol[band, 0:1] == tid_ref[...].astype(jnp.float32)
            out_ref[band, :] = jnp.where(same, 0.0, total * normal)

    for k in range(steps):
        for j in range(1, far + 1):
            got = cbuf.at[k, :, columns(behind(me, j))]
            remote(got, c_y_s.at[j - 1, k], c_y_r.at[j - 1, k], ahead(j)).wait_recv()
            go(remote(got, c_fw_s.at[j - 1, k], c_fw_r.at[j - 1, k], sib))
        remote(cbuf.at[k, :, columns(sib)], c_sib_s.at[k], c_sib_r.at[k], sib).wait_recv()
        for j in range(1, far + 1):
            got = cbuf.at[k, :, columns(behind(sib, j))]
            remote(got, c_fw_s.at[j - 1, k], c_fw_r.at[j - 1, k], sib).wait_recv()
        if k == 0:
            for copy in g_loads:
                copy.wait()

        for n in range(train // TILE):
            tile = slice(n * TILE, (n + 1) * TILE)
            scores = lax.dot_general(cbuf[k], gbuf[tile, :], NT, preferred_element_type=jnp.float32)
            sbuf[k, :, tile] = scores.astype(jnp.bfloat16)
            for b in range(n_ex):
                @pl.when(fe == b // per_owner)
                def _():
                    spot = (b % per_owner) * steps + k
                    own[spot * CHUNK:(spot + 1) * CHUNK, tile] = scores[b * CHUNK:(b + 1) * CHUNK]

        for b in range(n_ex):
            @pl.when(fe != b // per_owner)
            def _():
                z_copy(k, b).start()
        if k > 0:
            finish(k - 1)
    finish(steps - 1)

    for copy in sent:
        copy.wait_send()
    for k in range(steps):
        for b in range(n_ex):
            @pl.when(fe != b // per_owner)
            def _():
                z_copy(k, b).wait_send()


def local(n_ex, n_feat, queries, train_grads, preconditioner, query_ids, train_ids, layer_seeds):
    rows, feats = queries.shape
    layers, prow, width = preconditioner.shape
    train = train_grads.shape[0]
    out_rows = query_ids.shape[0]
    steps = rows // CHUNK
    far = max(n_ex // 2 - 1, 1)
    dma = pltpu.SemaphoreType.DMA
    any_space = pl.BlockSpec(memory_space=pl.ANY)
    vmem = pl.BlockSpec(memory_space=pltpu.VMEM)
    return pl.pallas_call(
        functools.partial(kernel, n_ex, n_feat),
        out_shape=jax.ShapeDtypeStruct((out_rows, train), jnp.float32),
        in_specs=[any_space, any_space, any_space, vmem, vmem, pl.BlockSpec(memory_space=pltpu.SMEM)],
        out_specs=vmem,
        scratch_shapes=[
            pltpu.VMEM((steps, n_ex * CHUNK, feats), jnp.bfloat16),
            pltpu.VMEM((steps, n_ex * CHUNK, feats), jnp.bfloat16),
            pltpu.VMEM((train, feats), jnp.bfloat16),
            pltpu.VMEM((layers, prow, width), jnp.bfloat16),
            pltpu.VMEM((steps, n_ex * CHUNK, train), jnp.bfloat16),
            pltpu.VMEM((n_feat, out_rows, train), jnp.bfloat16),
            pltpu.VMEM((out_rows, train), jnp.float32),
            pltpu.VMEM((out_rows, 128), jnp.float32),
            dma((steps,)), dma((layers,)), dma((n_ex * layers,)),
            dma((steps,)), dma((steps,)), dma((far, steps)), dma((far, steps)), dma((far, steps)), dma((far, steps)),
            dma((steps,)), dma((steps,)), dma((far, steps)), dma((far, steps)), dma((far, steps)), dma((far, steps)),
            dma((steps, n_ex)), dma((n_feat, steps * (n_ex // n_feat))),
        ],
        compiler_params=pltpu.CompilerParams(
            collective_id=0, has_side_effects=True, vmem_limit_bytes=56 * 1024 * 1024
        ),
        cost_estimate=pl.CostEstimate(
            flops=2 * n_ex * rows * feats * (prow + train),
            bytes_accessed=2 * feats * (rows + layers * prow // 2 + train),
            transcendentals=0,
        ),
    )(
        queries, train_grads, preconditioner,
        query_ids.reshape(1, -1), train_ids.reshape(1, -1), layer_seeds,
    )


def solution(mesh):
    in_specs = (
        P(("grp", "ex"), "feat"),
        P(("grp", "ex"), "feat"),
        P("feat", "ex", None),
        P(("grp", "feat")),
        P(("grp", "ex")),
        P("feat"),
    )
    out_specs = P(("grp", "feat"), "ex")
    body = functools.partial(local, mesh.shape["ex"], mesh.shape["feat"])
    return jax.shard_map(body, mesh=mesh, in_specs=in_specs, out_specs=out_specs, check_vma=False)
```

```python
import functools
import math

import jax
import jax.numpy as jnp
from jax import lax
from jax.experimental import pallas as pl
from jax.experimental.pallas import tpu as pltpu
from jax.sharding import PartitionSpec as P

CHUNK = 16
AHEAD = 2
TILE = 512
NT = (((1,), (1,)), ((), ()))


def sketch_sign_row(seed, width):
    feature = lax.broadcasted_iota(jnp.int32, (1, width), 1)
    hashed = seed + feature * 40503
    sixteen = jnp.full_like(hashed, 16)
    hashed = (hashed ^ lax.shift_right_logical(hashed, sixteen)) * 73244475
    hashed = (hashed ^ lax.shift_right_logical(hashed, sixteen)) * 73244475
    hashed = hashed ^ lax.shift_right_logical(hashed, sixteen)
    return (1 - 2 * (hashed & 1)).astype(jnp.float32).astype(jnp.bfloat16)


def kernel(
    n_ex, n_feat,
    q_hbm, g_hbm, p_hbm, qid_ref, tid_ref, seed_ref, out_ref,
    qbuf, cbuf, gbuf, pbuf, sbuf, zbuf, own, acc, qcol,
    load_q, load_p, load_g,
    q_sib_s, q_sib_r, q_y_s, q_y_r, q_fw_s, q_fw_r,
    c_sib_s, c_sib_r, c_y_s, c_y_r, c_fw_s, c_fw_r,
    z_s, z_r,
):
    rows, feats = q_hbm.shape
    layers, prow, width = p_hbm.shape
    train = g_hbm.shape[0]
    steps = rows // CHUNK
    part = layers * prow
    per_owner = n_ex // n_feat
    far = n_ex // 2 - 1
    me = lax.axis_index("ex")
    fe = lax.axis_index("feat")
    sib = me + 1 - 2 * lax.rem(me, 2)

    def block(k, e):
        return qbuf.at[k, pl.ds(pl.multiple_of(e * CHUNK, CHUNK), CHUNK)]

    def columns(e):
        return pl.ds(pl.multiple_of(e * part, 128), part)

    def ahead(j):
        return lax.rem(me + 2 * j, n_ex)

    def behind(e, j):
        return lax.rem(e + n_ex - 2 * j, n_ex)

    def remote(ref, send, recv, target):
        return pltpu.make_async_remote_copy(
            src_ref=ref, dst_ref=ref, send_sem=send, recv_sem=recv,
            device_id={"ex": target}, device_id_type=pl.DeviceIdType.MESH,
        )

    q_loads = [
        pltpu.make_async_copy(q_hbm.at[pl.ds(k * CHUNK, CHUNK)], block(k, me), load_q.at[k])
        for k in range(steps)
    ]
    p_loads = [
        pltpu.make_async_copy(p_hbm.at[l], pbuf.at[l], load_p.at[l]) for l in range(layers)
    ]
    g_loads = [
        pltpu.make_async_copy(
            g_hbm.at[:, pl.ds(l * width + e * prow, prow)],
            gbuf.at[:, pl.ds(e * part + l * prow, prow)],
            load_g.at[e * layers + l],
        )
        for e in range(n_ex)
        for l in range(layers)
    ]
    for copy in q_loads:
        copy.start()

    barrier = pltpu.get_barrier_semaphore()
    pl.semaphore_signal(barrier, inc=1, device_id={"ex": sib}, device_id_type=pl.DeviceIdType.MESH)
    for j in range(1, far + 1):
        pl.semaphore_signal(barrier, inc=1, device_id={"ex": ahead(j)}, device_id_type=pl.DeviceIdType.MESH)
    for d in range(1, n_feat):
        pl.semaphore_signal(
            barrier, inc=1, device_id={"feat": lax.rem(fe + d, n_feat)}, device_id_type=pl.DeviceIdType.MESH
        )

    signs = [sketch_sign_row(seed_ref[l], width) for l in range(layers)]
    eye = lax.broadcasted_iota(jnp.int32, (qid_ref.shape[1],) * 2, 0) == lax.broadcasted_iota(
        jnp.int32, (qid_ref.shape[1],) * 2, 1
    )
    ids = jnp.broadcast_to(qid_ref[...].astype(jnp.float32), eye.shape)
    qcol[...] = jnp.broadcast_to(
        jnp.sum(jnp.where(eye, ids, 0.0), axis=1, keepdims=True), qcol.shape
    )

    sent = []

    def go(copy):
        copy.start()
        sent.append(copy)

    def send_y(i):
        k = i % steps
        for j in range(1, far + 1):
            if i < steps:
                go(remote(block(k, me), q_y_s.at[j - 1, k], q_y_r.at[j - 1, k], ahead(j)))
            elif i < 2 * steps:
                mine = cbuf.at[k, :, columns(me)]
                go(remote(mine, c_y_s.at[j - 1, k], c_y_r.at[j - 1, k], ahead(j)))

    for k in range(steps):
        q_loads[k].wait()
        place = pl.ds(pl.multiple_of(me * CHUNK, CHUNK), CHUNK)
        for l in range(layers):
            lanes = slice(l * width, (l + 1) * width)
            qbuf[k, place, lanes] = qbuf[k, place, lanes] * signs[l]
        if k == 0:
            pl.semaphore_wait(barrier, far + n_feat)
        if k < AHEAD:
            send_y(k)
        go(remote(block(k, me), q_sib_s.at[k], q_sib_r.at[k], sib))

    for copy in p_loads + g_loads:
        copy.start()

    for k in range(steps):
        for j in range(1, far + 1):
            src = behind(me, j)
            remote(block(k, src), q_y_s.at[j - 1, k], q_y_r.at[j - 1, k], ahead(j)).wait_recv()
            if j == far:
                send_y(k + AHEAD)
            go(remote(block(k, src), q_fw_s.at[j - 1, k], q_fw_r.at[j - 1, k], sib))
        remote(block(k, sib), q_sib_s.at[k], q_sib_r.at[k], sib).wait_recv()
        for j in range(1, far + 1):
            src = behind(sib, j)
            remote(block(k, src), q_fw_s.at[j - 1, k], q_fw_r.at[j - 1, k], sib).wait_recv()
        if k == 0:
            for copy in p_loads:
                copy.wait()
        for l in range(layers):
            got = lax.dot_general(
                pbuf[l], qbuf[k, :, l * width:(l + 1) * width], NT, preferred_element_type=jnp.float32
            ).T
            cbuf[k, :, pl.ds(pl.multiple_of(me * part + l * prow, 128), prow)] = got.astype(jnp.bfloat16)
        mine = cbuf.at[k, :, columns(me)]
        go(remote(mine, c_sib_s.at[k], c_sib_r.at[k], sib))

    normal = 1.0 / math.sqrt(n_feat * layers * width)

    def z_copy(k, b):
        owner, spot = b // per_owner, (b % per_owner) * steps + k
        return pltpu.make_async_remote_copy(
            src_ref=sbuf.at[k, pl.ds(b * CHUNK, CHUNK)],
            dst_ref=zbuf.at[fe, pl.ds(spot * CHUNK, CHUNK)],
            send_sem=z_s.at[k, b],
            recv_sem=z_r.at[fe, spot],
            device_id={"feat": owner},
            device_id_type=pl.DeviceIdType.MESH,
        )

    def finish(k):
        for m in range(per_owner):
            spot = m * steps + k
            band = pl.ds(spot * CHUNK, CHUNK)
            total = own[band, :]
            for d in range(1, n_feat):
                src = lax.rem(fe + d, n_feat)
                pltpu.make_async_remote_copy(
                    src_ref=zbuf.at[src, band], dst_ref=zbuf.at[src, band],
                    send_sem=z_s.at[k, m], recv_sem=z_r.at[src, spot],
                    device_id={"feat": src}, device_id_type=pl.DeviceIdType.MESH,
                ).wait_recv()
                total = total + zbuf[src, band, :].astype(jnp.float32)
            same = qcol[band, 0:1] == tid_ref[...].astype(jnp.float32)
            out_ref[band, :] = jnp.where(same, 0.0, total * normal)

    def product(k, lanes, tile):
        return lax.dot_general(gbuf[tile, lanes], cbuf[k, :, lanes], NT, preferred_element_type=jnp.float32)

    tiles = [slice(n * TILE, (n + 1) * TILE) for n in range(train // TILE)]
    chip = pl.ds(pl.multiple_of((me - lax.rem(me, 2)) * part, 128), 2 * part)

    for copy in g_loads:
        copy.wait()
    for k in range(steps):
        remote(cbuf.at[k, :, columns(sib)], c_sib_s.at[k], c_sib_r.at[k], sib).wait_recv()
        for tile in tiles:
            acc[tile, :] = product(k, chip, tile)
        for j in range(1, far + 1):
            got = cbuf.at[k, :, columns(behind(me, j))]
            remote(got, c_y_s.at[j - 1, k], c_y_r.at[j - 1, k], ahead(j)).wait_recv()
            if j == far:
                send_y(steps + k + AHEAD)
            go(remote(got, c_fw_s.at[j - 1, k], c_fw_r.at[j - 1, k], sib))
        for j in range(1, far + 1):
            for tile in tiles:
                acc[tile, :] += product(k, columns(behind(me, j)), tile)
        for j in range(1, far + 1):
            got = cbuf.at[k, :, columns(behind(sib, j))]
            remote(got, c_fw_s.at[j - 1, k], c_fw_r.at[j - 1, k], sib).wait_recv()
            for tile in tiles:
                scores = acc[tile, :] + product(k, columns(behind(sib, j)), tile)
                if j < far:
                    acc[tile, :] = scores
                    continue
                scores = scores.T
                sbuf[k, :, tile] = scores.astype(jnp.bfloat16)
                for b in range(n_ex):
                    @pl.when(fe == b // per_owner)
                    def _():
                        spot = (b % per_owner) * steps + k
                        own[spot * CHUNK:(spot + 1) * CHUNK, tile] = scores[b * CHUNK:(b + 1) * CHUNK]

        for b in range(n_ex):
            @pl.when(fe != b // per_owner)
            def _():
                z_copy(k, b).start()
        if k > 0:
            finish(k - 1)
    finish(steps - 1)

    for copy in sent:
        copy.wait_send()
    for k in range(steps):
        for b in range(n_ex):
            @pl.when(fe != b // per_owner)
            def _():
                z_copy(k, b).wait_send()


def local(n_ex, n_feat, queries, train_grads, preconditioner, query_ids, train_ids, layer_seeds):
    rows, feats = queries.shape
    layers, prow, width = preconditioner.shape
    train = train_grads.shape[0]
    out_rows = query_ids.shape[0]
    steps = rows // CHUNK
    far = max(n_ex // 2 - 1, 1)
    dma = pltpu.SemaphoreType.DMA
    any_space = pl.BlockSpec(memory_space=pl.ANY)
    vmem = pl.BlockSpec(memory_space=pltpu.VMEM)
    return pl.pallas_call(
        functools.partial(kernel, n_ex, n_feat),
        out_shape=jax.ShapeDtypeStruct((out_rows, train), jnp.float32),
        in_specs=[any_space, any_space, any_space, vmem, vmem, pl.BlockSpec(memory_space=pltpu.SMEM)],
        out_specs=vmem,
        scratch_shapes=[
            pltpu.VMEM((steps, n_ex * CHUNK, feats), jnp.bfloat16),
            pltpu.VMEM((steps, n_ex * CHUNK, feats), jnp.bfloat16),
            pltpu.VMEM((train, feats), jnp.bfloat16),
            pltpu.VMEM((layers, prow, width), jnp.bfloat16),
            pltpu.VMEM((steps, n_ex * CHUNK, train), jnp.bfloat16),
            pltpu.VMEM((n_feat, out_rows, train), jnp.bfloat16),
            pltpu.VMEM((out_rows, train), jnp.float32),
            pltpu.VMEM((train, n_ex * CHUNK), jnp.float32),
            pltpu.VMEM((out_rows, 128), jnp.float32),
            dma((steps,)), dma((layers,)), dma((n_ex * layers,)),
            dma((steps,)), dma((steps,)), dma((far, steps)), dma((far, steps)), dma((far, steps)), dma((far, steps)),
            dma((steps,)), dma((steps,)), dma((far, steps)), dma((far, steps)), dma((far, steps)), dma((far, steps)),
            dma((steps, n_ex)), dma((n_feat, steps * (n_ex // n_feat))),
        ],
        compiler_params=pltpu.CompilerParams(
            collective_id=0, has_side_effects=True, vmem_limit_bytes=56 * 1024 * 1024
        ),
        cost_estimate=pl.CostEstimate(
            flops=2 * n_ex * rows * feats * (prow + train),
            bytes_accessed=2 * feats * (rows + layers * prow // 2 + train),
            transcendentals=0,
        ),
    )(
        queries, train_grads, preconditioner,
        query_ids.reshape(1, -1), train_ids.reshape(1, -1), layer_seeds,
    )


def solution(mesh):
    in_specs = (
        P(("grp", "ex"), "feat"),
        P(("grp", "ex"), "feat"),
        P("feat", "ex", None),
        P(("grp", "feat")),
        P(("grp", "ex")),
        P("feat"),
    )
    out_specs = P(("grp", "feat"), "ex")
    body = functools.partial(local, mesh.shape["ex"], mesh.shape["feat"])
    return jax.shard_map(body, mesh=mesh, in_specs=in_specs, out_specs=out_specs, check_vma=False)
```

```python
import functools
import math

import jax
import jax.numpy as jnp
from jax import lax
from jax.experimental import pallas as pl
from jax.experimental.pallas import tpu as pltpu
from jax.sharding import PartitionSpec as P

CHUNK = 16
AHEAD = 3
TILE = 512
NT = (((1,), (1,)), ((), ()))


def sketch_sign_row(seed, width):
    feature = lax.broadcasted_iota(jnp.int32, (1, width), 1)
    hashed = seed + feature * 40503
    sixteen = jnp.full_like(hashed, 16)
    hashed = (hashed ^ lax.shift_right_logical(hashed, sixteen)) * 73244475
    hashed = (hashed ^ lax.shift_right_logical(hashed, sixteen)) * 73244475
    hashed = hashed ^ lax.shift_right_logical(hashed, sixteen)
    return (1 - 2 * (hashed & 1)).astype(jnp.float32).astype(jnp.bfloat16)


def kernel(
    n_ex, n_feat,
    q_hbm, g_hbm, p_hbm, qid_ref, tid_ref, seed_ref, out_ref,
    qbuf, cbuf, gbuf, pbuf, sbuf, zbuf, own, acc, qcol,
    load_q, load_p, load_g,
    q_sib_s, q_sib_r, q_y_s, q_y_r, q_fw_s, q_fw_r,
    c_sib_s, c_sib_r, c_y_s, c_y_r, c_fw_s, c_fw_r,
    z_s, z_r,
):
    rows, feats = q_hbm.shape
    layers, prow, width = p_hbm.shape
    train = g_hbm.shape[0]
    steps = rows // CHUNK
    part = layers * prow
    per_owner = n_ex // n_feat
    far = n_ex // 2 - 1
    me = lax.axis_index("ex")
    fe = lax.axis_index("feat")
    sib = me + 1 - 2 * lax.rem(me, 2)

    def block(k, e):
        return qbuf.at[k, pl.ds(pl.multiple_of(e * CHUNK, CHUNK), CHUNK)]

    def columns(e):
        return pl.ds(pl.multiple_of(e * part, 128), part)

    def ahead(j):
        return lax.rem(me + 2 * j, n_ex)

    def behind(e, j):
        return lax.rem(e + n_ex - 2 * j, n_ex)

    def remote(ref, send, recv, target):
        return pltpu.make_async_remote_copy(
            src_ref=ref, dst_ref=ref, send_sem=send, recv_sem=recv,
            device_id={"ex": target}, device_id_type=pl.DeviceIdType.MESH,
        )

    q_loads = [
        pltpu.make_async_copy(q_hbm.at[pl.ds(k * CHUNK, CHUNK)], block(k, me), load_q.at[k])
        for k in range(steps)
    ]
    p_loads = [
        pltpu.make_async_copy(p_hbm.at[l], pbuf.at[l], load_p.at[l]) for l in range(layers)
    ]
    g_loads = [
        pltpu.make_async_copy(
            g_hbm.at[:, pl.ds(l * width + e * prow, prow)],
            gbuf.at[:, pl.ds(e * part + l * prow, prow)],
            load_g.at[e * layers + l],
        )
        for e in range(n_ex)
        for l in range(layers)
    ]
    for copy in q_loads:
        copy.start()

    barrier = pltpu.get_barrier_semaphore()
    pl.semaphore_signal(barrier, inc=1, device_id={"ex": sib}, device_id_type=pl.DeviceIdType.MESH)
    for j in range(1, far + 1):
        pl.semaphore_signal(barrier, inc=1, device_id={"ex": ahead(j)}, device_id_type=pl.DeviceIdType.MESH)
    for d in range(1, n_feat):
        pl.semaphore_signal(
            barrier, inc=1, device_id={"feat": lax.rem(fe + d, n_feat)}, device_id_type=pl.DeviceIdType.MESH
        )

    signs = [sketch_sign_row(seed_ref[l], width) for l in range(layers)]
    eye = lax.broadcasted_iota(jnp.int32, (qid_ref.shape[1],) * 2, 0) == lax.broadcasted_iota(
        jnp.int32, (qid_ref.shape[1],) * 2, 1
    )
    ids = jnp.broadcast_to(qid_ref[...].astype(jnp.float32), eye.shape)
    qcol[...] = jnp.broadcast_to(
        jnp.sum(jnp.where(eye, ids, 0.0), axis=1, keepdims=True), qcol.shape
    )

    sent = []

    def go(copy):
        copy.start()
        sent.append(copy)

    def send_y(i):
        k = i % steps
        for j in range(1, far + 1):
            if i < steps:
                go(remote(block(k, me), q_y_s.at[j - 1, k], q_y_r.at[j - 1, k], ahead(j)))
            elif i < 2 * steps:
                mine = cbuf.at[k, :, columns(me)]
                go(remote(mine, c_y_s.at[j - 1, k], c_y_r.at[j - 1, k], ahead(j)))

    for k in range(steps):
        q_loads[k].wait()
        place = pl.ds(pl.multiple_of(me * CHUNK, CHUNK), CHUNK)
        for l in range(layers):
            lanes = slice(l * width, (l + 1) * width)
            qbuf[k, place, lanes] = qbuf[k, place, lanes] * signs[l]
        if k == 0:
            pl.semaphore_wait(barrier, far + n_feat)
        if k < AHEAD:
            send_y(k)
        go(remote(block(k, me), q_sib_s.at[k], q_sib_r.at[k], sib))

    for copy in p_loads + g_loads:
        copy.start()

    for k in range(steps):
        for j in range(1, far + 1):
            src = behind(me, j)
            remote(block(k, src), q_y_s.at[j - 1, k], q_y_r.at[j - 1, k], ahead(j)).wait_recv()
            if j == far:
                send_y(k + AHEAD)
            go(remote(block(k, src), q_fw_s.at[j - 1, k], q_fw_r.at[j - 1, k], sib))
        remote(block(k, sib), q_sib_s.at[k], q_sib_r.at[k], sib).wait_recv()
        for j in range(1, far + 1):
            src = behind(sib, j)
            remote(block(k, src), q_fw_s.at[j - 1, k], q_fw_r.at[j - 1, k], sib).wait_recv()
        if k == 0:
            for copy in p_loads:
                copy.wait()
        for l in range(layers):
            got = lax.dot_general(
                pbuf[l], qbuf[k, :, l * width:(l + 1) * width], NT, preferred_element_type=jnp.float32
            ).T
            cbuf[k, :, pl.ds(pl.multiple_of(me * part + l * prow, 128), prow)] = got.astype(jnp.bfloat16)
        mine = cbuf.at[k, :, columns(me)]
        go(remote(mine, c_sib_s.at[k], c_sib_r.at[k], sib))

    normal = 1.0 / math.sqrt(n_feat * layers * width)

    def z_copy(k, b):
        owner, spot = b // per_owner, (b % per_owner) * steps + k
        return pltpu.make_async_remote_copy(
            src_ref=sbuf.at[k, pl.ds(b * CHUNK, CHUNK)],
            dst_ref=zbuf.at[fe, pl.ds(spot * CHUNK, CHUNK)],
            send_sem=z_s.at[k, b],
            recv_sem=z_r.at[fe, spot],
            device_id={"feat": owner},
            device_id_type=pl.DeviceIdType.MESH,
        )

    def finish(k):
        for m in range(per_owner):
            spot = m * steps + k
            band = pl.ds(spot * CHUNK, CHUNK)
            total = own[band, :]
            for d in range(1, n_feat):
                src = lax.rem(fe + d, n_feat)
                pltpu.make_async_remote_copy(
                    src_ref=zbuf.at[src, band], dst_ref=zbuf.at[src, band],
                    send_sem=z_s.at[k, m], recv_sem=z_r.at[src, spot],
                    device_id={"feat": src}, device_id_type=pl.DeviceIdType.MESH,
                ).wait_recv()
                total = total + zbuf[src, band, :].astype(jnp.float32)
            same = qcol[band, 0:1] == tid_ref[...].astype(jnp.float32)
            out_ref[band, :] = jnp.where(same, 0.0, total * normal)

    def product(k, lanes, tile):
        return lax.dot_general(gbuf[tile, lanes], cbuf[k, :, lanes], NT, preferred_element_type=jnp.float32)

    tiles = [slice(n * TILE, (n + 1) * TILE) for n in range(train // TILE)]
    chip = pl.ds(pl.multiple_of((me - lax.rem(me, 2)) * part, 128), 2 * part)

    for copy in g_loads:
        copy.wait()
    for k in range(steps):
        remote(cbuf.at[k, :, columns(sib)], c_sib_s.at[k], c_sib_r.at[k], sib).wait_recv()
        for tile in tiles:
            acc[tile, :] = product(k, chip, tile)
        for j in range(1, far + 1):
            got = cbuf.at[k, :, columns(behind(me, j))]
            remote(got, c_y_s.at[j - 1, k], c_y_r.at[j - 1, k], ahead(j)).wait_recv()
            if j == far:
                send_y(steps + k + AHEAD)
            go(remote(got, c_fw_s.at[j - 1, k], c_fw_r.at[j - 1, k], sib))
        for j in range(1, far + 1):
            for tile in tiles:
                acc[tile, :] += product(k, columns(behind(me, j)), tile)
        for j in range(1, far + 1):
            got = cbuf.at[k, :, columns(behind(sib, j))]
            remote(got, c_fw_s.at[j - 1, k], c_fw_r.at[j - 1, k], sib).wait_recv()
            for tile in tiles:
                scores = acc[tile, :] + product(k, columns(behind(sib, j)), tile)
                if j < far:
                    acc[tile, :] = scores
                    continue
                scores = scores.T
                sbuf[k, :, tile] = scores.astype(jnp.bfloat16)
                for b in range(n_ex):
                    @pl.when(fe == b // per_owner)
                    def _():
                        spot = (b % per_owner) * steps + k
                        own[spot * CHUNK:(spot + 1) * CHUNK, tile] = scores[b * CHUNK:(b + 1) * CHUNK]

        for b in range(n_ex):
            @pl.when(fe != b // per_owner)
            def _():
                z_copy(k, b).start()
        if k > 1:
            finish(k - 2)
    for k in range(max(steps - 2, 0), steps):
        finish(k)

    for copy in sent:
        copy.wait_send()
    for k in range(steps):
        for b in range(n_ex):
            @pl.when(fe != b // per_owner)
            def _():
                z_copy(k, b).wait_send()


def local(n_ex, n_feat, queries, train_grads, preconditioner, query_ids, train_ids, layer_seeds):
    rows, feats = queries.shape
    layers, prow, width = preconditioner.shape
    train = train_grads.shape[0]
    out_rows = query_ids.shape[0]
    steps = rows // CHUNK
    far = max(n_ex // 2 - 1, 1)
    dma = pltpu.SemaphoreType.DMA
    any_space = pl.BlockSpec(memory_space=pl.ANY)
    vmem = pl.BlockSpec(memory_space=pltpu.VMEM)
    return pl.pallas_call(
        functools.partial(kernel, n_ex, n_feat),
        out_shape=jax.ShapeDtypeStruct((out_rows, train), jnp.float32),
        in_specs=[any_space, any_space, any_space, vmem, vmem, pl.BlockSpec(memory_space=pltpu.SMEM)],
        out_specs=vmem,
        scratch_shapes=[
            pltpu.VMEM((steps, n_ex * CHUNK, feats), jnp.bfloat16),
            pltpu.VMEM((steps, n_ex * CHUNK, feats), jnp.bfloat16),
            pltpu.VMEM((train, feats), jnp.bfloat16),
            pltpu.VMEM((layers, prow, width), jnp.bfloat16),
            pltpu.VMEM((steps, n_ex * CHUNK, train), jnp.bfloat16),
            pltpu.VMEM((n_feat, out_rows, train), jnp.bfloat16),
            pltpu.VMEM((out_rows, train), jnp.float32),
            pltpu.VMEM((train, n_ex * CHUNK), jnp.float32),
            pltpu.VMEM((out_rows, 128), jnp.float32),
            dma((steps,)), dma((layers,)), dma((n_ex * layers,)),
            dma((steps,)), dma((steps,)), dma((far, steps)), dma((far, steps)), dma((far, steps)), dma((far, steps)),
            dma((steps,)), dma((steps,)), dma((far, steps)), dma((far, steps)), dma((far, steps)), dma((far, steps)),
            dma((steps, n_ex)), dma((n_feat, steps * (n_ex // n_feat))),
        ],
        compiler_params=pltpu.CompilerParams(
            collective_id=0, has_side_effects=True, vmem_limit_bytes=56 * 1024 * 1024
        ),
        cost_estimate=pl.CostEstimate(
            flops=2 * n_ex * rows * feats * (prow + train),
            bytes_accessed=2 * feats * (rows + layers * prow // 2 + train),
            transcendentals=0,
        ),
    )(
        queries, train_grads, preconditioner,
        query_ids.reshape(1, -1), train_ids.reshape(1, -1), layer_seeds,
    )


def solution(mesh):
    in_specs = (
        P(("grp", "ex"), "feat"),
        P(("grp", "ex"), "feat"),
        P("feat", "ex", None),
        P(("grp", "feat")),
        P(("grp", "ex")),
        P("feat"),
    )
    out_specs = P(("grp", "feat"), "ex")
    body = functools.partial(local, mesh.shape["ex"], mesh.shape["feat"])
    return jax.shard_map(body, mesh=mesh, in_specs=in_specs, out_specs=out_specs, check_vma=False)
```
